32 devices in a mesh: groups: 2 (over y), expert: 16 (over z, x, core), head: 1.
Axes of the slice: x: 2, y: 2, z: 4, core: 2. Of those that a mesh axis runs over, the one named last changes fastest.
Arguments:
- tokens: bfloat16 [512, 2048], P(('groups', 'expert', 'head')), parts along dimension 0, may hold values from -6 to 6
- norm_gain: float32 [2048], replicated, may hold values from 0.1 to 1.9
- expert_ids: int32 [512, 8], P(('groups', 'expert', 'head')), parts along dimension 0, may hold values from 0 to 15, all different within a row; in each aligned block of 16 rows (0 to 15, 16 to 31, ...) at most 8 rows name the same one
- gate_values: float32 [512, 8], P(('groups', 'expert', 'head')), parts along dimension 0, may hold values from 0.1 to 1
- w_gate: bfloat16 [16, 2048, 768], P('expert', None, 'head'), may hold values from -0.125 to 0.125
- w_up: bfloat16 [16, 2048, 768], P('expert', None, 'head'), may hold values from -0.125 to 0.125
- w_down: bfloat16 [16, 2048, 768], P('expert', None, 'head'), may hold values from -0.21875 to 0.21875
Outputs:
- mixed: bfloat16 [512, 2048], P(('groups', 'expert', 'head')), parts along dimension 0
The draws below stay inside these ranges and needn't reach their ends.
There are 2 independent parts, one for each index of `groups`. The reference program is written for one: setup_inputs(seed, part) draws one part's arguments, and reference() takes and returns one part's arrays. A program takes and returns all parts, laid end to end along the dimension named above; an argument that names none is the same for every part. Nothing has to cross between parts.
Inputs may be any that keep to these rules, and one draw needn't show every extreme that they name: `expert_ids`: each row names 8 different experts. Among the 16 rows of one device no expert is named more than 8 times, a bound that some block reaches.
All inputs are finite; a program needn't handle non-finite values.
Results may differ from the reference program's by a relative error of at most 0.007.
Values may be sent and summed in bfloat16 or wider, within the bound.
A program may use at most 64 MiB of HBM per device.

```python
import math
import jax
import jax.numpy as jnp
import numpy as np
from jax import lax

D = 2048
FF = 768
TOPK = 8
TOK_DEV = 16
EXPERTS = 16
CAP = 8
TOKENS = 256
N_EXPERT = 16
N_HEAD = 1


def levels(key, extent, pieces, low, largest):
    def one(axis_at, parts):
        steps = jax.random.uniform(jax.random.fold_in(jax.random.fold_in(key, 6), axis_at), (parts,), jnp.float32, low / len(pieces), largest / len(pieces))
        return jnp.repeat(jnp.exp(steps), extent[axis_at] // parts).reshape((-1,) + (1,) * (len(extent) - axis_at - 1))

    loudness = one(*pieces[0])
    for cut in pieces[1:]:
        loudness = loudness * one(*cut)
    return loudness


def shared_out(own_key, own, number, rows, count, top, most, skew):
    ranking = jax.random.permutation(own_key, count)
    packed, common = load_shares(count, rows * top, most, skew, True), load_shares(count, rows * top, most, skew, False)
    places = jnp.arange(count)

    def named(sizes, turn):
        used = int((sizes > 0).sum())
        fixed = max(1, used // 4)
        moved = fixed + (places - fixed + turn * (used - fixed)) % max(1, count - fixed)
        return jnp.zeros((count,), jnp.int32).at[ranking[jnp.where(places < fixed, places, moved)]].set(jnp.asarray(sizes, jnp.int32))

    sizes = jnp.where(number % 4 == 0, named(packed, number // 4), named(common, number - number // 4 - 1))
    mixed = jax.random.permutation(jax.random.fold_in(own, 3), count)
    giver, receiver = mixed[0:count // 2 * 2:2], mixed[1:count // 2 * 2:2]
    margin = jnp.minimum(sizes[giver] - 1, most - sizes[receiver]) // 2
    margin = jnp.where((giver == ranking[0]) | (receiver == ranking[0]) | (sizes[receiver] == 0), 0, jnp.maximum(margin, 0))
    moved = jax.random.randint(jax.random.fold_in(own, 4), (count // 2,), 0, 1 << 20) % (margin + 1)
    sizes = sizes.at[giver].add(-moved).at[receiver].add(moved)
    labels = jnp.searchsorted(jnp.cumsum(sizes), jnp.arange(rows * top), side="right").astype(jnp.int32)
    listing = labels.reshape(top, rows).T
    listing = listing[jax.random.permutation(jax.random.fold_in(own, 1), rows)]
    turn = jax.random.randint(jax.random.fold_in(own, 2), (rows, 1), 0, top)
    return jnp.take_along_axis(listing, (jnp.arange(top)[None, :] + turn) % top, axis=1)


def load_shares(count, total, reach, slope, full):
    portions = [(1 << 20) // math.isqrt(grade ** slope) + 1 for grade in range(1, count + 1)]
    largest = reach if full else min(reach, max(-(-total // count), total * portions[0] // sum(portions)))
    least = 1 if total - largest >= count - 1 else 0
    counts, rest = [largest] + [least] * (count - 1), total - largest - least * (count - 1)
    while rest > 0:
        candidates = [i for i in range(1, count) if counts[i] < largest] or [i for i in range(1, count) if counts[i] < reach]
        mass, budget = sum([portions[i] for i in candidates]), rest
        for i in candidates:
            extra = min(reach - counts[i], max(1, budget * portions[i] // mass), rest)
            counts[i] = counts[i] + extra
            rest = rest - extra
    return np.array(counts)


def normal_values(own_key, extent, deviation, bound, split=(), kind=jnp.bfloat16):
    entries = deviation * jax.random.normal(own_key, extent, jnp.float32)
    if split:
        entries = entries * levels(own_key, extent, split, -0.22, 0.18)
    return jnp.clip(entries, -bound, bound).astype(kind)


def setup_inputs(seed: int = 0, part: int = 0) -> dict:
    keys = jax.random.split(jax.random.key(seed), 8)
    own_keys = jax.random.split(jax.random.fold_in(keys[7], part), 8)
    tokens = normal_values(own_keys[0], (TOKENS, D), 1.0, 6.0, ((0, 16),))
    norm_gain = jnp.clip(1.0 + 0.18 * jax.random.normal(keys[1], (D,), jnp.float32), 0.1, 1.9)
    expert_ids_keys = jax.random.split(jax.random.fold_in(own_keys[2], 1), TOKENS // TOK_DEV)
    expert_ids_turns = jax.random.permutation(jax.random.fold_in(own_keys[2], 3), TOKENS // TOK_DEV)
    expert_ids = jax.vmap(lambda own, number: shared_out(jax.random.fold_in(own_keys[2], 2), own, number, TOK_DEV, EXPERTS, TOPK, CAP, 2))(expert_ids_keys, expert_ids_turns).reshape((TOKENS, TOPK))
    gate_values = jnp.clip(0.1 + 0.9 * jax.random.uniform(own_keys[3], (TOKENS, TOPK), jnp.float32) ** levels(own_keys[3], (TOKENS, TOPK), ((0, 16),), -0.2, 0.2), 0.1, 1.0)
    w_gate = normal_values(keys[4], (EXPERTS, D, FF), D ** -0.5, 0.125, ((0, 16),))
    w_up = normal_values(keys[5], (EXPERTS, D, FF), D ** -0.5, 0.125, ((0, 16),))
    w_down = normal_values(keys[6], (EXPERTS, D, FF), FF ** -0.5, 0.21875, ((0, 16),))
    return dict(tokens=tokens, norm_gain=norm_gain, expert_ids=expert_ids, gate_values=gate_values, w_gate=w_gate, w_up=w_up, w_down=w_down)


def reference(tokens, norm_gain, expert_ids, gate_values, w_gate, w_up, w_down):
    tokens_f = tokens.astype(jnp.float32)
    scale = lax.rsqrt(lax.optimization_barrier(jnp.mean(tokens_f * tokens_f, axis=-1, keepdims=True)) + 1e-06)
    normed = (tokens_f * scale * norm_gain.astype(jnp.float32)[None, :]).astype(jnp.bfloat16)
    limit = N_EXPERT * N_HEAD * CAP

    def one_expert(carry, index):
        hit = expert_ids == index
        row_hit = jnp.any(hit, axis=1)
        weight = lax.optimization_barrier(jnp.sum(jnp.where(hit, gate_values, jnp.zeros_like(gate_values)), axis=1))
        count = jnp.sum(row_hit.astype(jnp.int32))
        picked = jnp.nonzero(row_hit, size=limit, fill_value=0)[0].astype(jnp.int32)
        valid = (jnp.arange(limit, dtype=jnp.int32) < count).astype(jnp.float32)
        chosen = normed[picked]
        gate = jnp.dot(chosen, w_gate[index], preferred_element_type=jnp.float32)
        upper = jnp.dot(chosen, w_up[index], preferred_element_type=jnp.float32)
        hidden = (jax.nn.silu(gate) * upper).astype(jnp.bfloat16)
        result = jnp.dot(hidden, w_down[index].T, preferred_element_type=jnp.float32).astype(jnp.bfloat16)
        term = result.astype(jnp.float32) * (weight[picked] * valid)[:, None]
        return (carry.at[picked].add(term), None)
    start = jnp.zeros((tokens.shape[0], tokens.shape[1]), jnp.float32)
    total, unused = lax.scan(one_expert, start, jnp.arange(EXPERTS, dtype=jnp.int32))
    return total.astype(jnp.bfloat16)
```

```python
import functools

import jax
import jax.numpy as jnp
from jax import lax
from jax.experimental import pallas as pl
from jax.experimental.pallas import tpu as pltpu
from jax.sharding import PartitionSpec as P


def expert_apply(rows_in, gate_part, up_part, down_part):
    gate = jnp.dot(rows_in, gate_part, preferred_element_type=jnp.float32)
    upper = jnp.dot(rows_in, up_part, preferred_element_type=jnp.float32)
    hidden = (jax.nn.silu(gate) * upper).astype(jnp.bfloat16)
    return lax.dot_general(
        hidden, down_part, (((1,), (1,)), ((), ())), preferred_element_type=jnp.float32
    )


def routed_device(tokens, norm_gain, expert_ids, gate_values, w_gate, w_up, w_down):
    rows, width = tokens.shape
    top = expert_ids.shape[1]
    expert_count = lax.axis_size("expert")
    capacity = max(2, top * rows // expert_count)
    tokens_f = tokens.astype(jnp.float32)
    scale = lax.rsqrt(jnp.mean(tokens_f * tokens_f, axis=-1, keepdims=True) + 1e-06)
    normed = (tokens_f * scale * norm_gain[None, :]).astype(jnp.bfloat16)
    flat_ids = expert_ids.reshape(-1)
    routes_here = flat_ids.shape[0]
    picks = (flat_ids[:, None] == jnp.arange(expert_count, dtype=jnp.int32)[None, :]).astype(
        jnp.bfloat16
    )
    order = jnp.arange(routes_here, dtype=jnp.int32)
    lower = (order[:, None] > order[None, :]).astype(jnp.bfloat16)
    earlier = jnp.dot(lower, picks, preferred_element_type=jnp.float32)
    slot = jnp.sum(earlier * picks.astype(jnp.float32), axis=1).astype(jnp.int32)
    position = flat_ids * capacity + slot
    place = (
        position[:, None] == jnp.arange(expert_count * capacity, dtype=jnp.int32)[None, :]
    ).astype(jnp.bfloat16)
    repeated = jnp.repeat(normed, top, axis=0)
    outgoing = lax.dot_general(
        place, repeated, (((0,), (0,)), ((), ())), preferred_element_type=jnp.float32
    )
    outgoing = outgoing.astype(jnp.bfloat16).reshape(expert_count, capacity, width)
    received = lax.all_to_all(outgoing, "expert", split_axis=0, concat_axis=0, tiled=True)
    count = received.shape[1]
    paired = lax.all_gather(received, "head", axis=0, tiled=True)
    partial_value = expert_apply(paired.reshape(-1, width), w_gate[0], w_up[0], w_down[0])
    partial_value = partial_value.reshape(paired.shape[0], count, width)
    result = lax.psum_scatter(partial_value, "head", scatter_dimension=0, tiled=True).astype(
        jnp.bfloat16
    )
    answered = lax.all_to_all(result, "expert", split_axis=0, concat_axis=0, tiled=True)
    per_route = jnp.dot(place, answered.reshape(-1, width), preferred_element_type=jnp.float32)
    weighted = per_route.reshape(rows, top, width) * gate_values[:, :, None]
    return jnp.sum(weighted, axis=1).astype(jnp.bfloat16)


MESH = pl.DeviceIdType.MESH
GATE = 128
CHUNKS = 4


def gathered_kernel(
    tokens_ref, gain_ref, ids_ref, gates_ref, wg_hbm, wu_hbm, wd_hbm, out_ref,
    buf, wg, wu, wd, acc, hid, part, c_src, c_dst, x_src, x_dst, z_src, z_dst,
    w_sem, ag_send, ag_recv, rs_send, rs_recv,
):
    rows, width = tokens_ref.shape
    hidden = wg.shape[1]
    every = buf.shape[0]
    layers = every // (4 * rows)
    quarter, half = every // 4, every // 2
    cut = width // CHUNKS

    group, head = lax.axis_index("groups"), lax.axis_index("head")
    me = lax.axis_index("expert")
    z, x, c = me // 4, (me // 2) % 2, me % 2

    def device(dz, dx, dc):
        zt = (z + dz + layers) % layers
        xt = (x + dx) % 2
        ct = (c + dc) % 2
        return (group, zt * 4 + xt * 2 + ct, head)

    weight_copies = []
    for k in range(CHUNKS):
        span = pl.ds(k * cut, cut)
        for i, (src, dst) in enumerate(((wg_hbm, wg), (wu_hbm, wu))):
            copy = pltpu.make_async_copy(src.at[0, span], dst.at[span], w_sem.at[i, k])
            copy.start()
            weight_copies.append(copy)
    down_copies = []
    for k in range(CHUNKS):
        span = pl.ds(k * cut, cut)
        copy = pltpu.make_async_copy(wd_hbm.at[0, span], wd.at[span], w_sem.at[2, k])
        copy.start()
        down_copies.append(copy)

    partners = [device(dz, 0, 0) for dz in range(1, layers)] + [device(0, 1, 0), device(0, 0, 1)]
    barrier = pltpu.get_barrier_semaphore()
    for partner in partners:
        pl.semaphore_signal(barrier, inc=1, device_id=partner, device_id_type=MESH)

    tokens_f = tokens_ref[...].astype(jnp.float32)
    scale = lax.rsqrt(jnp.mean(tokens_f * tokens_f, axis=-1, keepdims=True) + 1e-06)
    buf[0:rows, GATE:] = (tokens_f * scale * gain_ref[...]).astype(jnp.bfloat16)
    lane = lax.broadcasted_iota(jnp.int32, (rows, GATE), 1)
    slot = lane % 16
    ids, gates = ids_ref[...], gates_ref[...]
    spread = jnp.zeros((rows, GATE), jnp.float32)
    for k in range(ids.shape[1]):
        spread += jnp.where(ids[:, k : k + 1] == slot, gates[:, k : k + 1], 0.0)
    first = spread.astype(jnp.bfloat16).astype(jnp.float32)
    rest = spread - first
    second = rest.astype(jnp.bfloat16).astype(jnp.float32)
    third = rest - second
    parts = jnp.where(lane < 16, first, jnp.where(lane < 32, second, jnp.where(lane < 48, third, 0.0)))
    buf[0:rows, 0:GATE] = parts.astype(jnp.bfloat16)

    pl.semaphore_wait(barrier, len(partners))

    def columns(k):
        return pl.ds(0, GATE + cut) if k == 0 else pl.ds(GATE + k * cut, cut)

    started = []

    def send(src, dst, sems, k, i, target):
        send_sems, recv_sems = sems
        copy = pltpu.make_async_remote_copy(
            src_ref=src, dst_ref=dst, send_sem=send_sems.at[k, i], recv_sem=recv_sems.at[k, i],
            device_id=target, device_id_type=MESH,
        )
        copy.start()
        started.append(copy)
        return copy

    gather_sems, scatter_sems = (ag_send, ag_recv), (rs_send, rs_recv)

    def gather(k, i, at, size, to, target):
        span = columns(k)
        return send(
            buf.at[pl.ds(at, size), span], buf.at[pl.ds(to, size), span], gather_sems, k, i, target
        )

    along_z, along_x, along_c = {}, {}, {}
    for k in range(CHUNKS):
        along_z[k] = [
            gather(k, dz - 1, 0, rows, dz * rows, device(dz, 0, 0)) for dz in range(1, layers)
        ]
        along_x[k] = [gather(k, 3, 0, rows, quarter, device(0, 1, 0))]

    def multiply(k):
        weight_copies[2 * k].wait()
        weight_copies[2 * k + 1].wait()
        lhs = buf[:, GATE + k * cut : GATE + (k + 1) * cut]
        for w, base in ((wg, 0), (wu, hidden)):
            for n in range(0, hidden, 256):
                value = jnp.dot(
                    lhs, w[k * cut : (k + 1) * cut, n : n + 256], preferred_element_type=jnp.float32
                )
                at = slice(base + n, base + n + 256)
                if k == 0:
                    acc[:, at] = value
                else:
                    acc[:, at] += value

    for step in range(CHUNKS + 2):
        if step < CHUNKS:
            k = step
            for copy in along_z[k]:
                copy.wait_recv()
            along_x[k].append(
                gather(k, 4, rows, quarter - rows, quarter + rows, device(0, 1, 0))
            )
            along_c[k] = [gather(k, 5, 0, quarter, half, device(0, 0, 1))]
        if 0 <= step - 1 < CHUNKS:
            k = step - 1
            for copy in along_x[k]:
                copy.wait_recv()
            along_c[k].append(gather(k, 6, quarter, quarter, half + quarter, device(0, 0, 1)))
        if 0 <= step - 2 < CHUNKS:
            k = step - 2
            for copy in along_c[k]:
                copy.wait_recv()
            multiply(k)

    gate, upper = acc[:, 0:hidden], acc[:, hidden:]
    hid[...] = (gate / (1.0 + jnp.exp(-gate)) * upper).astype(jnp.bfloat16)
    wide = lax.broadcasted_iota(jnp.int32, (every, GATE), 1)
    mine = jnp.where(wide % 16 == me, buf[:, 0:GATE].astype(jnp.float32), 0.0)
    weight = jnp.sum(mine, axis=1, keepdims=True)

    to_core, to_x, to_z = {}, {}, {}
    for step in range(CHUNKS + 3):
        if step < CHUNKS:
            k = step
            down_copies[k].wait()
            for n in range(k * cut, (k + 1) * cut, 256):
                at = slice(n, n + 256)
                value = lax.dot_general(
                    hid[...], wd[at, :], (((1,), (1,)), ((), ())),
                    preferred_element_type=jnp.float32,
                )
                value = value * weight
                c_src[:, at] = value[half:].astype(jnp.bfloat16)
                part[:, at] = value[:half]
            span = pl.ds(k * cut, cut)
            to_core[k] = send(
                c_src.at[:, span], c_dst.at[:, span], scatter_sems, k, 0, device(0, 0, 1)
            )
        if 0 <= step - 1 < CHUNKS:
            k = step - 1
            at, span = slice(k * cut, (k + 1) * cut), pl.ds(k * cut, cut)
            to_core[k].wait_recv()
            x_src[:, at] = (
                part[quarter:, at] + c_dst[quarter:, at].astype(jnp.float32)
            ).astype(jnp.bfloat16)
            to_x[k] = send(x_src.at[:, span], x_dst.at[:, span], scatter_sems, k, 1, device(0, 1, 0))
            part[:quarter, at] += c_dst[:quarter, at].astype(jnp.float32)
        if 0 <= step - 2 < CHUNKS:
            k = step - 2
            at, span = slice(k * cut, (k + 1) * cut), pl.ds(k * cut, cut)
            to_x[k].wait_recv()
            z_src[:, at] = (
                part[rows:quarter, at] + x_dst[rows:, at].astype(jnp.float32)
            ).astype(jnp.bfloat16)
            to_z[k] = [
                send(
                    z_src.at[pl.ds((dz - 1) * rows, rows), span],
                    z_dst.at[pl.ds((dz - 1) * rows, rows), span],
                    scatter_sems, k, 1 + dz, device(-dz, 0, 0),
                )
                for dz in range(1, layers)
            ]
            part[:rows, at] += x_dst[:rows, at].astype(jnp.float32)
        if 0 <= step - 3 < CHUNKS:
            k = step - 3
            at = slice(k * cut, (k + 1) * cut)
            for copy in to_z[k]:
                copy.wait_recv()
            total = part[:rows, at]
            for dz in range(layers - 1):
                total += z_dst[dz * rows : (dz + 1) * rows, at].astype(jnp.float32)
            out_ref[:, at] = total.astype(jnp.bfloat16)

    for copy in started:
        copy.wait_send()


def gathered_device(tokens, norm_gain, expert_ids, gate_values, w_gate, w_up, w_down):
    rows, width = tokens.shape
    hidden = w_gate.shape[2]
    every = rows * lax.axis_size("expert")
    bf16, f32 = jnp.bfloat16, jnp.float32
    vmem, hbm = pl.BlockSpec(memory_space=pltpu.VMEM), pl.BlockSpec(memory_space=pl.ANY)
    return pl.pallas_call(
        gathered_kernel,
        out_shape=jax.ShapeDtypeStruct((rows, width), bf16),
        in_specs=[vmem] * 4 + [hbm] * 3,
        out_specs=vmem,
        scratch_shapes=[
            pltpu.VMEM((every, GATE + width), bf16),
            pltpu.VMEM((width, hidden), bf16),
            pltpu.VMEM((width, hidden), bf16),
            pltpu.VMEM((width, hidden), bf16),
            pltpu.VMEM((every, 2 * hidden), f32),
            pltpu.VMEM((every, hidden), bf16),
            pltpu.VMEM((every // 2, width), f32),
            pltpu.VMEM((every // 2, width), bf16),
            pltpu.VMEM((every // 2, width), bf16),
            pltpu.VMEM((every // 4, width), bf16),
            pltpu.VMEM((every // 4, width), bf16),
            pltpu.VMEM((every // 4 - rows, width), bf16),
            pltpu.VMEM((every // 4 - rows, width), bf16),
            pltpu.SemaphoreType.DMA((3, CHUNKS)),
            pltpu.SemaphoreType.DMA((CHUNKS, 7)),
            pltpu.SemaphoreType.DMA((CHUNKS, 7)),
            pltpu.SemaphoreType.DMA((CHUNKS, 5)),
            pltpu.SemaphoreType.DMA((CHUNKS, 5)),
        ],
        compiler_params=pltpu.CompilerParams(
            collective_id=0, has_side_effects=True, vmem_limit_bytes=40 * 1024 * 1024
        ),
    )(tokens, norm_gain.reshape(1, width), expert_ids, gate_values, w_gate, w_up, w_down)


def solution(mesh):
    in_specs = (
        P(("groups", "expert", "head"), None),
        P(),
        P(("groups", "expert", "head"), None),
        P(("groups", "expert", "head"), None),
        P("expert", None, "head"),
        P("expert", None, "head"),
        P("expert", None, "head"),
    )
    out_specs = P(("groups", "expert", "head"), None)
    experts = mesh.shape["expert"]
    dense = mesh.shape["head"] == 1 and experts == 16
    per_device = gathered_device if dense else routed_device
    return jax.shard_map(
        per_device, mesh=mesh, in_specs=in_specs, out_specs=out_specs, check_vma=False
    )
```

```python
import functools

import jax
import jax.numpy as jnp
from jax import lax
from jax.experimental import pallas as pl
from jax.experimental.pallas import tpu as pltpu
from jax.sharding import PartitionSpec as P


def expert_apply(rows_in, gate_part, up_part, down_part):
    gate = jnp.dot(rows_in, gate_part, preferred_element_type=jnp.float32)
    upper = jnp.dot(rows_in, up_part, preferred_element_type=jnp.float32)
    hidden = (jax.nn.silu(gate) * upper).astype(jnp.bfloat16)
    return lax.dot_general(
        hidden, down_part, (((1,), (1,)), ((), ())), preferred_element_type=jnp.float32
    )


def routed_device(tokens, norm_gain, expert_ids, gate_values, w_gate, w_up, w_down):
    rows, width = tokens.shape
    top = expert_ids.shape[1]
    expert_count = lax.axis_size("expert")
    capacity = max(2, top * rows // expert_count)
    tokens_f = tokens.astype(jnp.float32)
    scale = lax.rsqrt(jnp.mean(tokens_f * tokens_f, axis=-1, keepdims=True) + 1e-06)
    normed = (tokens_f * scale * norm_gain[None, :]).astype(jnp.bfloat16)
    flat_ids = expert_ids.reshape(-1)
    routes_here = flat_ids.shape[0]
    picks = (flat_ids[:, None] == jnp.arange(expert_count, dtype=jnp.int32)[None, :]).astype(
        jnp.bfloat16
    )
    order = jnp.arange(routes_here, dtype=jnp.int32)
    lower = (order[:, None] > order[None, :]).astype(jnp.bfloat16)
    earlier = jnp.dot(lower, picks, preferred_element_type=jnp.float32)
    slot = jnp.sum(earlier * picks.astype(jnp.float32), axis=1).astype(jnp.int32)
    position = flat_ids * capacity + slot
    place = (
        position[:, None] == jnp.arange(expert_count * capacity, dtype=jnp.int32)[None, :]
    ).astype(jnp.bfloat16)
    repeated = jnp.repeat(normed, top, axis=0)
    outgoing = lax.dot_general(
        place, repeated, (((0,), (0,)), ((), ())), preferred_element_type=jnp.float32
    )
    outgoing = outgoing.astype(jnp.bfloat16).reshape(expert_count, capacity, width)
    received = lax.all_to_all(outgoing, "expert", split_axis=0, concat_axis=0, tiled=True)
    count = received.shape[1]
    paired = lax.all_gather(received, "head", axis=0, tiled=True)
    partial_value = expert_apply(paired.reshape(-1, width), w_gate[0], w_up[0], w_down[0])
    partial_value = partial_value.reshape(paired.shape[0], count, width)
    result = lax.psum_scatter(partial_value, "head", scatter_dimension=0, tiled=True).astype(
        jnp.bfloat16
    )
    answered = lax.all_to_all(result, "expert", split_axis=0, concat_axis=0, tiled=True)
    per_route = jnp.dot(place, answered.reshape(-1, width), preferred_element_type=jnp.float32)
    weighted = per_route.reshape(rows, top, width) * gate_values[:, :, None]
    return jnp.sum(weighted, axis=1).astype(jnp.bfloat16)


MESH = pl.DeviceIdType.MESH
GATE = 128
TILE = 256


def gathered_kernel(
    tokens_hbm, gain_hbm, ids_hbm, gates_hbm, wg_hbm, wu_hbm, wd_hbm, out_ref,
    tokens_ref, gain_ref, ids_ref, gates_ref,
    buf, wg, wu, wd, hid, part, c_src, c_dst, x_src, x_dst, z_src, z_dst,
    zb_src, zb_dst, xb_src, xb_dst,
    in_sem, w_sem, send_sem, recv_sem,
):
    rows, width = tokens_ref.shape
    hidden = wg.shape[1]
    half = 8 * rows
    bf16, f32 = jnp.bfloat16, jnp.float32

    group, head = lax.axis_index("groups"), lax.axis_index("head")
    me = lax.axis_index("expert")
    z, x, c = me // 4, (me // 2) % 2, me % 2
    layer = [z, z + 1 - 2 * (z % 2), (z + 2) % 4, 3 - z]

    def device(far=0, dx=0, dc=0):
        return (group, layer[far] * 4 + ((x + dx) % 2) * 2 + (c + dc) % 2, head)

    partners = [device(3), device(2), device(1), device(0, 1), device(0, 0, 1)]
    barrier = pltpu.get_barrier_semaphore()
    for partner in partners:
        pl.semaphore_signal(barrier, inc=1, device_id=partner, device_id_type=MESH)

    pairs = (
        (tokens_hbm, tokens_ref), (gain_hbm, gain_ref), (ids_hbm, ids_ref), (gates_hbm, gates_ref)
    )
    inputs = [pltpu.make_async_copy(s, d, in_sem.at[i]) for i, (s, d) in enumerate(pairs)]
    for copy in inputs:
        copy.start()
    weights = []
    for i, (src, dst) in enumerate(((wg_hbm, wg), (wu_hbm, wu), (wd_hbm, wd))):
        for k in range(4):
            span = pl.ds(k * (width // 4), width // 4)
            weights.append(pltpu.make_async_copy(src.at[0, span], dst.at[span], w_sem.at[i, k]))
    for copy in weights:
        copy.start()

    for copy in inputs:
        copy.wait()
    tokens_f = tokens_ref[...].astype(f32)
    scale = lax.rsqrt(jnp.mean(tokens_f * tokens_f, axis=-1, keepdims=True) + 1e-06)
    buf[0:rows, GATE:] = (tokens_f * scale * gain_ref[...]).astype(bf16)
    line = lax.broadcasted_iota(jnp.int32, (GATE, rows), 0)
    ids, gates = ids_ref[...], gates_ref[...]
    spread = jnp.zeros((GATE, rows), f32)
    for k in range(ids.shape[0]):
        spread += jnp.where(ids[k : k + 1, :] == line % 16, gates[k : k + 1, :], 0.0)
    first = spread.astype(bf16).astype(f32)
    rest = spread - first
    middle = rest.astype(bf16).astype(f32)
    third = rest - middle
    split = jnp.where(
        line < 16, first, jnp.where(line < 32, middle, jnp.where(line < 48, third, 0.0))
    )
    unit = lax.broadcasted_iota(jnp.int32, (rows, rows), 0) == lax.broadcasted_iota(
        jnp.int32, (rows, rows), 1
    )
    buf[0:rows, 0:GATE] = lax.dot_general(
        unit.astype(f32).astype(bf16), split.astype(bf16), (((1,), (1,)), ((), ())),
        preferred_element_type=f32,
    ).astype(bf16)

    pl.semaphore_wait(barrier, len(partners))

    started = []

    def send(src, dst, target):
        i = len(started)
        copy = pltpu.make_async_remote_copy(
            src_ref=src, dst_ref=dst, send_sem=send_sem.at[i], recv_sem=recv_sem.at[i],
            device_id=target, device_id_type=MESH,
        )
        copy.start()
        started.append(copy)
        return copy

    def gather(at, size, to, target, span=None):
        span = pl.ds(0, GATE + width) if span is None else span
        return send(buf.at[pl.ds(at, size), span], buf.at[pl.ds(to, size), span], target)

    def arrive(copies):
        for copy in copies:
            copy.wait_recv()

    two, four, mid = 2 * rows, 4 * rows, width // 2
    first_half, second_half = pl.ds(0, GATE + mid), pl.ds(GATE + mid, mid)
    place = {1: rows, 3: half, 2: half + rows}
    x_second = gather(0, rows, two, device(0, 1), second_half)
    z_first = {f: gather(0, rows, place[f], device(f), first_half) for f in (1, 3, 2)}
    x_first = [gather(0, rows, two, device(0, 1), first_half)]
    z_second = {f: [gather(0, rows, place[f], device(f), second_half)] for f in (2, 3, 1)}
    x_second.wait_recv()
    for f in (2, 3, 1):
        z_second[f].append(gather(two, rows, place[f] + two, device(f), second_half))
    far_x = []
    z_first[1].wait_recv()
    x_first.append(gather(rows, rows, two + rows, device(0, 1), first_half))
    for f in (3, 2):
        z_first[f].wait_recv()
        far_x.append(gather(place[f], rows, place[f] + two, device(0, 1), first_half))
    arrive(x_first)
    arrive(z_second[1])
    near_c = gather(0, four, four, device(0, 0, 1))
    for copy in weights:
        copy.wait()
    near_c.wait_recv()

    def project(h):
        at = slice(h * half, (h + 1) * half)
        for n in range(0, hidden, TILE):
            lhs = buf[at, GATE:]
            gate = jnp.dot(lhs, wg[:, n : n + TILE], preferred_element_type=f32)
            upper = jnp.dot(lhs, wu[:, n : n + TILE], preferred_element_type=f32)
            hid[at, n : n + TILE] = (gate / (1.0 + jnp.exp(-gate)) * upper).astype(bf16)
        wide = lax.broadcasted_iota(jnp.int32, (half, GATE), 1)
        mine = jnp.where(wide % 16 == me, buf[at, 0:GATE].astype(f32), 0.0)
        return jnp.sum(mine, axis=1, keepdims=True)

    def answer(h, weight, lo):
        mine = slice(h * four, (h + 1) * four)
        for n in range(lo, lo + mid, TILE):
            value = lax.dot_general(
                hid[h * half : (h + 1) * half, :], wd[n : n + TILE, :], (((1,), (1,)), ((), ())),
                preferred_element_type=f32,
            )
            value = value * weight
            c_src[mine, n : n + TILE] = value[four:].astype(bf16)
            part[mine, n : n + TILE] = value[:four]
        block = (pl.ds(h * four, four), pl.ds(lo, mid))
        return send(c_src.at[block], c_dst.at[block], device(0, 0, 1))

    def cross(h):
        base = h * four
        x_src[h * two : (h + 1) * two, :] = (
            part[base + two : base + four, :mid] + c_dst[base + two : base + four, :mid].astype(f32)
        ).astype(bf16)
        block = pl.ds(h * two, two)
        copy = send(x_src.at[block], x_dst.at[block], device(0, 1))
        part[base : base + two, :mid] += c_dst[base : base + two, :mid].astype(f32)
        return copy

    def along_first(far):
        at = {1: rows, 3: four, 2: four + rows}[far]
        got = {1: rows, 3: two, 2: two + rows}[far]
        out = slice((far - 1) * rows, far * rows)
        z_src[out, :] = (
            part[at : at + rows, :mid] + x_dst[got : got + rows, :].astype(f32)
        ).astype(bf16)
        block = pl.ds((far - 1) * rows, rows)
        return send(z_src.at[block], z_dst.at[block], device(far))

    def along_second(far):
        at = {1: rows, 3: four, 2: four + rows}[far]
        base = (far - 1) * two
        for i in range(2):
            row = slice(at + i * two, at + i * two + rows)
            zb_src[base + i * rows : base + (i + 1) * rows, :] = (
                part[row, mid:] + c_dst[row, mid:].astype(f32)
            ).astype(bf16)
        block = pl.ds(base, two)
        return send(zb_src.at[block], zb_dst.at[block], device(far))

    near_weight = project(0)
    arrive(far_x)
    arrive(z_second[3] + z_second[2])
    far_c = gather(half, four, half + four, device(0, 0, 1))
    near_back = [answer(0, near_weight, lo) for lo in (mid, 0)]
    far_c.wait_recv()
    far_weight = project(1)
    far_back = [answer(1, far_weight, mid)]
    near_back[0].wait_recv()
    second = {1: along_second(1)}
    near_back[1].wait_recv()
    near_cross = cross(0)
    far_back.append(answer(1, far_weight, 0))
    far_back[0].wait_recv()
    for far in (2, 3):
        second[far] = along_second(far)
    far_back[1].wait_recv()
    far_cross = cross(1)
    near_cross.wait_recv()
    last = [along_first(1)]
    part[0:rows, :mid] += x_dst[0:rows, :].astype(f32)
    own = [
        part[i * two : i * two + rows, mid:] + c_dst[i * two : i * two + rows, mid:].astype(f32)
        for i in range(2)
    ]
    for far in (1, 3, 2):
        second[far].wait_recv()
        for i in range(2):
            at = (far - 1) * two + i * rows
            own[i] += zb_dst[at : at + rows, :].astype(f32)
    xb_src[...] = own[1].astype(bf16)
    second_cross = send(xb_src, xb_dst, device(0, 1))
    far_cross.wait_recv()
    last.extend([along_first(2), along_first(3)])
    second_cross.wait_recv()
    out_ref[:, mid:] = (own[0] + xb_dst[...].astype(f32)).astype(bf16)
    arrive(last)
    total = part[0:rows, :mid]
    for i in range(3):
        total += z_dst[i * rows : (i + 1) * rows, :].astype(f32)
    out_ref[:, :mid] = total.astype(bf16)

    for copy in started:
        copy.wait_send()


def gathered_device(tokens, norm_gain, expert_ids, gate_values, w_gate, w_up, w_down):
    rows, width = tokens.shape
    top = expert_ids.shape[1]
    hidden = w_gate.shape[2]
    every = rows * 16
    bf16, f32 = jnp.bfloat16, jnp.float32
    vmem, hbm = pl.BlockSpec(memory_space=pltpu.VMEM), pl.BlockSpec(memory_space=pl.ANY)
    copies, mid = 29, width // 2
    return pl.pallas_call(
        gathered_kernel,
        out_shape=jax.ShapeDtypeStruct((rows, width), bf16),
        in_specs=[hbm] * 7,
        out_specs=vmem,
        scratch_shapes=[
            pltpu.VMEM((rows, width), bf16),
            pltpu.VMEM((1, width), f32),
            pltpu.VMEM((top, rows), jnp.int32),
            pltpu.VMEM((top, rows), f32),
            pltpu.VMEM((every, GATE + width), bf16),
            pltpu.VMEM((width, hidden), bf16),
            pltpu.VMEM((width, hidden), bf16),
            pltpu.VMEM((width, hidden), bf16),
            pltpu.VMEM((every, hidden), bf16),
            pltpu.VMEM((every // 2, width), f32),
            pltpu.VMEM((every // 2, width), bf16),
            pltpu.VMEM((every // 2, width), bf16),
            pltpu.VMEM((every // 4, mid), bf16),
            pltpu.VMEM((every // 4, mid), bf16),
            pltpu.VMEM((3 * rows, mid), bf16),
            pltpu.VMEM((3 * rows, mid), bf16),
            pltpu.VMEM((6 * rows, mid), bf16),
            pltpu.VMEM((6 * rows, mid), bf16),
            pltpu.VMEM((rows, mid), bf16),
            pltpu.VMEM((rows, mid), bf16),
            pltpu.SemaphoreType.DMA((4,)),
            pltpu.SemaphoreType.DMA((3, 4)),
            pltpu.SemaphoreType.DMA((copies,)),
            pltpu.SemaphoreType.DMA((copies,)),
        ],
        compiler_params=pltpu.CompilerParams(
            collective_id=0, has_side_effects=True, vmem_limit_bytes=61 * 1024 * 1024
        ),
    )(tokens, norm_gain.reshape(1, width), expert_ids.T, gate_values.T, w_gate, w_up, w_down)


def solution(mesh):
    in_specs = (
        P(("groups", "expert", "head"), None),
        P(),
        P(("groups", "expert", "head"), None),
        P(("groups", "expert", "head"), None),
        P("expert", None, "head"),
        P("expert", None, "head"),
        P("expert", None, "head"),
    )
    out_specs = P(("groups", "expert", "head"), None)
    experts = mesh.shape["expert"]
    dense = mesh.shape["head"] == 1 and experts == 16
    per_device = gathered_device if dense else routed_device
    return jax.shard_map(
        per_device, mesh=mesh, in_specs=in_specs, out_specs=out_specs, check_vma=False
    )
```

```python
import functools

import jax
import jax.numpy as jnp
from jax import lax
from jax.experimental import pallas as pl
from jax.experimental.pallas import tpu as pltpu
from jax.sharding import PartitionSpec as P


def expert_apply(rows_in, gate_part, up_part, down_part):
    gate = jnp.dot(rows_in, gate_part, preferred_element_type=jnp.float32)
    upper = jnp.dot(rows_in, up_part, preferred_element_type=jnp.float32)
    hidden = (jax.nn.silu(gate) * upper).astype(jnp.bfloat16)
    return lax.dot_general(
        hidden, down_part, (((1,), (1,)), ((), ())), preferred_element_type=jnp.float32
    )


def routed_device(tokens, norm_gain, expert_ids, gate_values, w_gate, w_up, w_down):
    rows, width = tokens.shape
    top = expert_ids.shape[1]
    expert_count = lax.axis_size("expert")
    capacity = max(2, top * rows // expert_count)
    tokens_f = tokens.astype(jnp.float32)
    scale = lax.rsqrt(jnp.mean(tokens_f * tokens_f, axis=-1, keepdims=True) + 1e-06)
    normed = (tokens_f * scale * norm_gain[None, :]).astype(jnp.bfloat16)
    flat_ids = expert_ids.reshape(-1)
    routes_here = flat_ids.shape[0]
    picks = (flat_ids[:, None] == jnp.arange(expert_count, dtype=jnp.int32)[None, :]).astype(
        jnp.bfloat16
    )
    order = jnp.arange(routes_here, dtype=jnp.int32)
    lower = (order[:, None] > order[None, :]).astype(jnp.bfloat16)
    earlier = jnp.dot(lower, picks, preferred_element_type=jnp.float32)
    slot = jnp.sum(earlier * picks.astype(jnp.float32), axis=1).astype(jnp.int32)
    position = flat_ids * capacity + slot
    place = (
        position[:, None] == jnp.arange(expert_count * capacity, dtype=jnp.int32)[None, :]
    ).astype(jnp.bfloat16)
    repeated = jnp.repeat(normed, top, axis=0)
    outgoing = lax.dot_general(
        place, repeated, (((0,), (0,)), ((), ())), preferred_element_type=jnp.float32
    )
    outgoing = outgoing.astype(jnp.bfloat16).reshape(expert_count, capacity, width)
    received = lax.all_to_all(outgoing, "expert", split_axis=0, concat_axis=0, tiled=True)
    count = received.shape[1]
    paired = lax.all_gather(received, "head", axis=0, tiled=True)
    partial_value = expert_apply(paired.reshape(-1, width), w_gate[0], w_up[0], w_down[0])
    partial_value = partial_value.reshape(paired.shape[0], count, width)
    result = lax.psum_scatter(partial_value, "head", scatter_dimension=0, tiled=True).astype(
        jnp.bfloat16
    )
    answered = lax.all_to_all(result, "expert", split_axis=0, concat_axis=0, tiled=True)
    per_route = jnp.dot(place, answered.reshape(-1, width), preferred_element_type=jnp.float32)
    weighted = per_route.reshape(rows, top, width) * gate_values[:, :, None]
    return jnp.sum(weighted, axis=1).astype(jnp.bfloat16)


MESH = pl.DeviceIdType.MESH
GATE = 128
FIRST = 6
TILE = 256


def gathered_kernel(
    tokens_hbm, gain_hbm, ids_hbm, gates_hbm, wg_hbm, wu_hbm, wd_hbm, out_ref,
    tokens_ref, gain_ref, ids_ref, gates_ref,
    buf, wg, wu, wd, hid, part, c_src, c_dst, x_src, x_dst, z_src, z_dst,
    zb_src, zb_dst, xb_src, xb_dst,
    in_sem, w_sem, send_sem, recv_sem,
):
    rows, width = tokens_ref.shape
    hidden = wg.shape[1]
    half = 8 * rows
    bf16, f32 = jnp.bfloat16, jnp.float32

    group, head = lax.axis_index("groups"), lax.axis_index("head")
    me = lax.axis_index("expert")
    z, x, c = me // 4, (me // 2) % 2, me % 2
    layer = [z, z + 1 - 2 * (z % 2), (z + 2) % 4, 3 - z]

    def device(far=0, dx=0, dc=0):
        return (group, layer[far] * 4 + ((x + dx) % 2) * 2 + (c + dc) % 2, head)

    partners = [device(3), device(2), device(1), device(0, 1), device(0, 0, 1)]
    barrier = pltpu.get_barrier_semaphore()
    for partner in partners:
        pl.semaphore_signal(barrier, inc=1, device_id=partner, device_id_type=MESH)

    pairs = (
        (tokens_hbm, tokens_ref), (gain_hbm, gain_ref), (ids_hbm, ids_ref), (gates_hbm, gates_ref)
    )
    inputs = [pltpu.make_async_copy(s, d, in_sem.at[i]) for i, (s, d) in enumerate(pairs)]
    for copy in inputs:
        copy.start()
    weights = []
    for i, (src, dst) in enumerate(((wg_hbm, wg), (wu_hbm, wu), (wd_hbm, wd))):
        for k in range(4):
            span = pl.ds(k * (width // 4), width // 4)
            weights.append(pltpu.make_async_copy(src.at[0, span], dst.at[span], w_sem.at[i, k]))

    for copy in inputs:
        copy.wait()
    tokens_f = tokens_ref[...].astype(f32)
    scale = lax.rsqrt(jnp.mean(tokens_f * tokens_f, axis=-1, keepdims=True) + 1e-06)
    buf[0:rows, GATE:] = (tokens_f * scale * gain_ref[...]).astype(bf16)
    line = lax.broadcasted_iota(jnp.int32, (GATE, rows), 0)
    ids, gates = ids_ref[...], gates_ref[...]
    spread = jnp.zeros((GATE, rows), f32)
    for k in range(ids.shape[0]):
        spread += jnp.where(ids[k : k + 1, :] == line % 16, gates[k : k + 1, :], 0.0)
    first = spread.astype(bf16).astype(f32)
    rest = spread - first
    middle = rest.astype(bf16).astype(f32)
    third = rest - middle
    split = jnp.where(
        line < 16, first, jnp.where(line < 32, middle, jnp.where(line < 48, third, 0.0))
    )
    unit = lax.broadcasted_iota(jnp.int32, (rows, rows), 0) == lax.broadcasted_iota(
        jnp.int32, (rows, rows), 1
    )
    buf[0:rows, 0:GATE] = lax.dot_general(
        unit.astype(f32).astype(bf16), split.astype(bf16), (((1,), (1,)), ((), ())),
        preferred_element_type=f32,
    ).astype(bf16)

    pl.semaphore_wait(barrier, len(partners))

    started = []

    def send(src, dst, target):
        i = len(started)
        copy = pltpu.make_async_remote_copy(
            src_ref=src, dst_ref=dst, send_sem=send_sem.at[i], recv_sem=recv_sem.at[i],
            device_id=target, device_id_type=MESH,
        )
        copy.start()
        started.append(copy)
        return copy

    def gather(at, size, to, target, span=None):
        span = pl.ds(0, GATE + width) if span is None else span
        return send(buf.at[pl.ds(at, size), span], buf.at[pl.ds(to, size), span], target)

    def arrive(copies):
        for copy in copies:
            copy.wait_recv()

    two, four, mid = 2 * rows, 4 * rows, width * FIRST // 8
    tail = width - mid
    first_half, second_half = pl.ds(0, GATE + mid), pl.ds(GATE + mid, tail)
    place = {1: rows, 3: half, 2: half + rows}
    x_second = gather(0, rows, two, device(0, 1), second_half)
    z_first = {f: gather(0, rows, place[f], device(f), first_half) for f in (1, 3, 2)}
    x_first = [gather(0, rows, two, device(0, 1), first_half)]
    z_second = {f: [gather(0, rows, place[f], device(f), second_half)] for f in (2, 3, 1)}
    for copy in weights:
        copy.start()
    x_second.wait_recv()
    for f in (2, 3, 1):
        z_second[f].append(gather(two, rows, place[f] + two, device(f), second_half))
    far_x = []
    z_first[1].wait_recv()
    x_first.append(gather(rows, rows, two + rows, device(0, 1), first_half))
    for f in (3, 2):
        z_first[f].wait_recv()
        far_x.append(gather(place[f], rows, place[f] + two, device(0, 1), first_half))
    arrive(x_first)
    arrive(z_second[1])
    near_c = gather(0, four, four, device(0, 0, 1))
    for copy in weights:
        copy.wait()
    near_c.wait_recv()

    def project(h):
        at = slice(h * half, (h + 1) * half)
        for n in range(0, hidden, TILE):
            lhs = buf[at, GATE:]
            gate = jnp.dot(lhs, wg[:, n : n + TILE], preferred_element_type=f32)
            upper = jnp.dot(lhs, wu[:, n : n + TILE], preferred_element_type=f32)
            hid[at, n : n + TILE] = (gate / (1.0 + jnp.exp(-gate)) * upper).astype(bf16)
        wide = lax.broadcasted_iota(jnp.int32, (half, GATE), 1)
        mine = jnp.where(wide % 16 == me, buf[at, 0:GATE].astype(f32), 0.0)
        return jnp.sum(mine, axis=1, keepdims=True)

    def answer(h, weight, lo):
        mine = slice(h * four, (h + 1) * four)
        size = tail if lo else mid
        for n in range(lo, lo + size, TILE):
            value = lax.dot_general(
                hid[h * half : (h + 1) * half, :], wd[n : n + TILE, :], (((1,), (1,)), ((), ())),
                preferred_element_type=f32,
            )
            value = value * weight
            c_src[mine, n : n + TILE] = value[four:].astype(bf16)
            part[mine, n : n + TILE] = value[:four]
        block = (pl.ds(h * four, four), pl.ds(lo, size))
        return send(c_src.at[block], c_dst.at[block], device(0, 0, 1))

    def cross(h):
        base = h * four
        x_src[h * two : (h + 1) * two, :] = (
            part[base + two : base + four, :mid] + c_dst[base + two : base + four, :mid].astype(f32)
        ).astype(bf16)
        block = pl.ds(h * two, two)
        copy = send(x_src.at[block], x_dst.at[block], device(0, 1))
        part[base : base + two, :mid] += c_dst[base : base + two, :mid].astype(f32)
        return copy

    def along_first(far):
        at = {1: rows, 3: four, 2: four + rows}[far]
        got = {1: rows, 3: two, 2: two + rows}[far]
        out = slice((far - 1) * rows, far * rows)
        z_src[out, :] = (
            part[at : at + rows, :mid] + x_dst[got : got + rows, :].astype(f32)
        ).astype(bf16)
        block = pl.ds((far - 1) * rows, rows)
        return send(z_src.at[block], z_dst.at[block], device(far))

    def along_second(far):
        at = {1: rows, 3: four, 2: four + rows}[far]
        base = (far - 1) * two
        for i in range(2):
            row = slice(at + i * two, at + i * two + rows)
            zb_src[base + i * rows : base + (i + 1) * rows, :] = (
                part[row, mid:] + c_dst[row, mid:].astype(f32)
            ).astype(bf16)
        block = pl.ds(base, two)
        return send(zb_src.at[block], zb_dst.at[block], device(far))

    near_weight = project(0)
    arrive(far_x)
    arrive(z_second[3] + z_second[2])
    far_c = gather(half, four, half + four, device(0, 0, 1))
    near_back = [answer(0, near_weight, lo) for lo in (mid, 0)]
    far_c.wait_recv()
    far_weight = project(1)
    far_back = [answer(1, far_weight, mid)]
    near_back[0].wait_recv()
    second = {1: along_second(1)}
    near_back[1].wait_recv()
    near_cross = cross(0)
    far_back.append(answer(1, far_weight, 0))
    far_back[0].wait_recv()
    for far in (2, 3):
        second[far] = along_second(far)
    far_back[1].wait_recv()
    far_cross = cross(1)
    near_cross.wait_recv()
    last = [along_first(1)]
    part[0:rows, :mid] += x_dst[0:rows, :].astype(f32)
    own = [
        part[i * two : i * two + rows, mid:] + c_dst[i * two : i * two + rows, mid:].astype(f32)
        for i in range(2)
    ]
    for far in (1, 3, 2):
        second[far].wait_recv()
        for i in range(2):
            at = (far - 1) * two + i * rows
            own[i] += zb_dst[at : at + rows, :].astype(f32)
    xb_src[...] = own[1].astype(bf16)
    second_cross = send(xb_src, xb_dst, device(0, 1))
    far_cross.wait_recv()
    last.extend([along_first(2), along_first(3)])
    second_cross.wait_recv()
    out_ref[:, mid:] = (own[0] + xb_dst[...].astype(f32)).astype(bf16)
    arrive(last)
    total = part[0:rows, :mid]
    for i in range(3):
        total += z_dst[i * rows : (i + 1) * rows, :].astype(f32)
    out_ref[:, :mid] = total.astype(bf16)

    for copy in started:
        copy.wait_send()


def gathered_device(tokens, norm_gain, expert_ids, gate_values, w_gate, w_up, w_down):
    rows, width = tokens.shape
    top = expert_ids.shape[1]
    hidden = w_gate.shape[2]
    every = rows * 16
    bf16, f32 = jnp.bfloat16, jnp.float32
    vmem, hbm = pl.BlockSpec(memory_space=pltpu.VMEM), pl.BlockSpec(memory_space=pl.ANY)
    copies, mid = 29, width * FIRST // 8
    tail = width - mid
    return pl.pallas_call(
        gathered_kernel,
        out_shape=jax.ShapeDtypeStruct((rows, width), bf16),
        in_specs=[hbm] * 7,
        out_specs=vmem,
        scratch_shapes=[
            pltpu.VMEM((rows, width), bf16),
            pltpu.VMEM((1, width), f32),
            pltpu.VMEM((top, rows), jnp.int32),
            pltpu.VMEM((top, rows), f32),
            pltpu.VMEM((every, GATE + width), bf16),
            pltpu.VMEM((width, hidden), bf16),
            pltpu.VMEM((width, hidden), bf16),
            pltpu.VMEM((width, hidden), bf16),
            pltpu.VMEM((every, hidden), bf16),
            pltpu.VMEM((every // 2, width), f32),
            pltpu.VMEM((every // 2, width), bf16),
            pltpu.VMEM((every // 2, width), bf16),
            pltpu.VMEM((every // 4, mid), bf16),
            pltpu.VMEM((every // 4, mid), bf16),
            pltpu.VMEM((3 * rows, mid), bf16),
            pltpu.VMEM((3 * rows, mid), bf16),
            pltpu.VMEM((6 * rows, tail), bf16),
            pltpu.VMEM((6 * rows, tail), bf16),
            pltpu.VMEM((rows, tail), bf16),
            pltpu.VMEM((rows, tail), bf16),
            pltpu.SemaphoreType.DMA((4,)),
            pltpu.SemaphoreType.DMA((3, 4)),
            pltpu.SemaphoreType.DMA((copies,)),
            pltpu.SemaphoreType.DMA((copies,)),
        ],
        compiler_params=pltpu.CompilerParams(
            collective_id=0, has_side_effects=True, vmem_limit_bytes=61 * 1024 * 1024
        ),
    )(tokens, norm_gain.reshape(1, width), expert_ids.T, gate_values.T, w_gate, w_up, w_down)


def solution(mesh):
    in_specs = (
        P(("groups", "expert", "head"), None),
        P(),
        P(("groups", "expert", "head"), None),
        P(("groups", "expert", "head"), None),
        P("expert", None, "head"),
        P("expert", None, "head"),
        P("expert", None, "head"),
    )
    out_specs = P(("groups", "expert", "head"), None)
    experts = mesh.shape["expert"]
    dense = mesh.shape["head"] == 1 and experts == 16
    per_device = gathered_device if dense else routed_device
    return jax.shard_map(
        per_device, mesh=mesh, in_specs=in_specs, out_specs=out_specs, check_vma=False
    )
```

```python
import functools

import jax
import jax.numpy as jnp
from jax import lax
from jax.experimental import pallas as pl
from jax.experimental.pallas import tpu as pltpu
from jax.sharding import PartitionSpec as P


def expert_apply(rows_in, gate_part, up_part, down_part):
    gate = jnp.dot(rows_in, gate_part, preferred_element_type=jnp.float32)
    upper = jnp.dot(rows_in, up_part, preferred_element_type=jnp.float32)
    hidden = (jax.nn.silu(gate) * upper).astype(jnp.bfloat16)
    return lax.dot_general(
        hidden, down_part, (((1,), (1,)), ((), ())), preferred_element_type=jnp.float32
    )


def routed_device(tokens, norm_gain, expert_ids, gate_values, w_gate, w_up, w_down):
    rows, width = tokens.shape
    top = expert_ids.shape[1]
    expert_count = lax.axis_size("expert")
    capacity = max(2, top * rows // expert_count)
    tokens_f = tokens.astype(jnp.float32)
    scale = lax.rsqrt(jnp.mean(tokens_f * tokens_f, axis=-1, keepdims=True) + 1e-06)
    normed = (tokens_f * scale * norm_gain[None, :]).astype(jnp.bfloat16)
    flat_ids = expert_ids.reshape(-1)
    routes_here = flat_ids.shape[0]
    picks = (flat_ids[:, None] == jnp.arange(expert_count, dtype=jnp.int32)[None, :]).astype(
        jnp.bfloat16
    )
    order = jnp.arange(routes_here, dtype=jnp.int32)
    lower = (order[:, None] > order[None, :]).astype(jnp.bfloat16)
    earlier = jnp.dot(lower, picks, preferred_element_type=jnp.float32)
    slot = jnp.sum(earlier * picks.astype(jnp.float32), axis=1).astype(jnp.int32)
    position = flat_ids * capacity + slot
    place = (
        position[:, None] == jnp.arange(expert_count * capacity, dtype=jnp.int32)[None, :]
    ).astype(jnp.bfloat16)
    repeated = jnp.repeat(normed, top, axis=0)
    outgoing = lax.dot_general(
        place, repeated, (((0,), (0,)), ((), ())), preferred_element_type=jnp.float32
    )
    outgoing = outgoing.astype(jnp.bfloat16).reshape(expert_count, capacity, width)
    received = lax.all_to_all(outgoing, "expert", split_axis=0, concat_axis=0, tiled=True)
    count = received.shape[1]
    paired = lax.all_gather(received, "head", axis=0, tiled=True)
    partial_value = expert_apply(paired.reshape(-1, width), w_gate[0], w_up[0], w_down[0])
    partial_value = partial_value.reshape(paired.shape[0], count, width)
    result = lax.psum_scatter(partial_value, "head", scatter_dimension=0, tiled=True).astype(
        jnp.bfloat16
    )
    answered = lax.all_to_all(result, "expert", split_axis=0, concat_axis=0, tiled=True)
    per_route = jnp.dot(place, answered.reshape(-1, width), preferred_element_type=jnp.float32)
    weighted = per_route.reshape(rows, top, width) * gate_values[:, :, None]
    return jnp.sum(weighted, axis=1).astype(jnp.bfloat16)


MESH = pl.DeviceIdType.MESH
GATE = 128
FIRST = 6
TILE = 256


def gathered_kernel(
    tokens_hbm, gain_hbm, ids_hbm, gates_hbm, wg_hbm, wu_hbm, wd_hbm, out_ref,
    tokens_ref, gain_ref, ids_ref, gates_ref,
    buf, wg, wu, wd, hid, part, c_src, c_dst, x_src, x_dst, z_src, z_dst,
    zb_src, zb_dst, xb_src, xb_dst,
    in_sem, w_sem, send_sem, recv_sem,
):
    rows, width = tokens_ref.shape
    hidden = wg.shape[1]
    half = 8 * rows
    bf16, f32 = jnp.bfloat16, jnp.float32

    group, head = lax.axis_index("groups"), lax.axis_index("head")
    me = lax.axis_index("expert")
    z, x, c = me // 4, (me // 2) % 2, me % 2
    layer = [z, z + 1 - 2 * (z % 2), (z + 2) % 4, 3 - z]

    def device(far=0, dx=0, dc=0):
        return (group, layer[far] * 4 + ((x + dx) % 2) * 2 + (c + dc) % 2, head)

    partners = [device(3), device(2), device(1), device(0, 1), device(0, 0, 1)]
    barrier = pltpu.get_barrier_semaphore()
    for partner in partners:
        pl.semaphore_signal(barrier, inc=1, device_id=partner, device_id_type=MESH)

    pairs = (
        (tokens_hbm, tokens_ref), (gain_hbm, gain_ref), (ids_hbm, ids_ref), (gates_hbm, gates_ref)
    )
    inputs = [pltpu.make_async_copy(s, d, in_sem.at[i]) for i, (s, d) in enumerate(pairs)]
    for copy in inputs:
        copy.start()
    weights = []
    for i, (src, dst) in enumerate(((wg_hbm, wg), (wu_hbm, wu), (wd_hbm, wd))):
        for k in range(4):
            span = pl.ds(k * (width // 4), width // 4)
            weights.append(pltpu.make_async_copy(src.at[0, span], dst.at[span], w_sem.at[i, k]))

    for copy in inputs:
        copy.wait()
    tokens_f = tokens_ref[...].astype(f32)
    scale = lax.rsqrt(jnp.mean(tokens_f * tokens_f, axis=-1, keepdims=True) + 1e-06)
    buf[0:rows, GATE:] = (tokens_f * scale * gain_ref[...]).astype(bf16)
    line = lax.broadcasted_iota(jnp.int32, (GATE, rows), 0)
    ids, gates = ids_ref[...], gates_ref[...]
    spread = jnp.zeros((GATE, rows), f32)
    for k in range(ids.shape[0]):
        spread += jnp.where(ids[k : k + 1, :] == line % 16, gates[k : k + 1, :], 0.0)
    first = spread.astype(bf16).astype(f32)
    rest = spread - first
    middle = rest.astype(bf16).astype(f32)
    third = rest - middle
    split = jnp.where(
        line < 16, first, jnp.where(line < 32, middle, jnp.where(line < 48, third, 0.0))
    )
    unit = lax.broadcasted_iota(jnp.int32, (rows, rows), 0) == lax.broadcasted_iota(
        jnp.int32, (rows, rows), 1
    )
    buf[0:rows, 0:GATE] = lax.dot_general(
        unit.astype(f32).astype(bf16), split.astype(bf16), (((1,), (1,)), ((), ())),
        preferred_element_type=f32,
    ).astype(bf16)

    pl.semaphore_wait(barrier, len(partners))

    started = []

    def send(src, dst, target):
        i = len(started)
        copy = pltpu.make_async_remote_copy(
            src_ref=src, dst_ref=dst, send_sem=send_sem.at[i], recv_sem=recv_sem.at[i],
            device_id=target, device_id_type=MESH,
        )
        copy.start()
        started.append(copy)
        return copy

    def gather(at, size, to, target, span=None):
        span = pl.ds(0, GATE + width) if span is None else span
        return send(buf.at[pl.ds(at, size), span], buf.at[pl.ds(to, size), span], target)

    def arrive(copies):
        for copy in copies:
            copy.wait_recv()

    two, four, mid = 2 * rows, 4 * rows, width * FIRST // 8
    tail = width - mid
    first_half, second_half = pl.ds(0, GATE + mid), pl.ds(GATE + mid, tail)
    place = {1: rows, 3: half, 2: half + rows}
    x_second = gather(0, rows, two, device(0, 1), second_half)
    z_first = {f: gather(0, rows, place[f], device(f), first_half) for f in (2, 3, 1)}
    x_first = [gather(0, rows, two, device(0, 1), first_half)]
    z_second = {f: [gather(0, rows, place[f], device(f), second_half)] for f in (2, 3, 1)}
    for copy in weights:
        copy.start()
    x_second.wait_recv()
    for f in (2, 3, 1):
        z_second[f].append(gather(two, rows, place[f] + two, device(f), second_half))
    far_x = []
    z_first[1].wait_recv()
    x_first.append(gather(rows, rows, two + rows, device(0, 1), first_half))
    for f in (3, 2):
        z_first[f].wait_recv()
        far_x.append(gather(place[f], rows, place[f] + two, device(0, 1), first_half))
    arrive(x_first)
    arrive(z_second[1])
    near_c = gather(0, four, four, device(0, 0, 1))
    for copy in weights:
        copy.wait()
    near_c.wait_recv()

    def project(h):
        at = slice(h * half, (h + 1) * half)
        for n in range(0, hidden, TILE):
            lhs = buf[at, GATE:]
            gate = jnp.dot(lhs, wg[:, n : n + TILE], preferred_element_type=f32)
            upper = jnp.dot(lhs, wu[:, n : n + TILE], preferred_element_type=f32)
            hid[at, n : n + TILE] = (gate / (1.0 + jnp.exp(-gate)) * upper).astype(bf16)
        wide = lax.broadcasted_iota(jnp.int32, (half, GATE), 1)
        mine = jnp.where(wide % 16 == me, buf[at, 0:GATE].astype(f32), 0.0)
        return jnp.sum(mine, axis=1, keepdims=True)

    def answer(h, weight, lo):
        mine = slice(h * four, (h + 1) * four)
        size = tail if lo else mid
        for n in range(lo, lo + size, TILE):
            value = lax.dot_general(
                hid[h * half : (h + 1) * half, :], wd[n : n + TILE, :], (((1,), (1,)), ((), ())),
                preferred_element_type=f32,
            )
            value = value * weight
            c_src[mine, n : n + TILE] = value[four:].astype(bf16)
            part[mine, n : n + TILE] = value[:four]
        block = (pl.ds(h * four, four), pl.ds(lo, size))
        return send(c_src.at[block], c_dst.at[block], device(0, 0, 1))

    def cross(h):
        base = h * four
        x_src[h * two : (h + 1) * two, :] = (
            part[base + two : base + four, :mid] + c_dst[base + two : base + four, :mid].astype(f32)
        ).astype(bf16)
        block = pl.ds(h * two, two)
        copy = send(x_src.at[block], x_dst.at[block], device(0, 1))
        part[base : base + two, :mid] += c_dst[base : base + two, :mid].astype(f32)
        return copy

    def along_first(far):
        at = {1: rows, 3: four, 2: four + rows}[far]
        got = {1: rows, 3: two, 2: two + rows}[far]
        out = slice((far - 1) * rows, far * rows)
        z_src[out, :] = (
            part[at : at + rows, :mid] + x_dst[got : got + rows, :].astype(f32)
        ).astype(bf16)
        block = pl.ds((far - 1) * rows, rows)
        return send(z_src.at[block], z_dst.at[block], device(far))

    def along_second(far):
        at = {1: rows, 3: four, 2: four + rows}[far]
        base = (far - 1) * two
        for i in range(2):
            row = slice(at + i * two, at + i * two + rows)
            zb_src[base + i * rows : base + (i + 1) * rows, :] = (
                part[row, mid:] + c_dst[row, mid:].astype(f32)
            ).astype(bf16)
        block = pl.ds(base, two)
        return send(zb_src.at[block], zb_dst.at[block], device(far))

    near_weight = project(0)
    arrive(far_x)
    arrive(z_second[3] + z_second[2])
    far_c = gather(half, four, half + four, device(0, 0, 1))
    near_back = [answer(0, near_weight, lo) for lo in (mid, 0)]
    far_c.wait_recv()
    far_weight = project(1)
    far_back = [answer(1, far_weight, mid)]
    near_back[0].wait_recv()
    second = {1: along_second(1)}
    near_back[1].wait_recv()
    near_cross = cross(0)
    far_back.append(answer(1, far_weight, 0))
    far_back[0].wait_recv()
    for far in (2, 3):
        second[far] = along_second(far)
    far_back[1].wait_recv()
    far_cross = cross(1)
    near_cross.wait_recv()
    last = [along_first(1)]
    part[0:rows, :mid] += x_dst[0:rows, :].astype(f32)
    own = [
        part[i * two : i * two + rows, mid:] + c_dst[i * two : i * two + rows, mid:].astype(f32)
        for i in range(2)
    ]
    for far in (1, 3, 2):
        second[far].wait_recv()
        for i in range(2):
            at = (far - 1) * two + i * rows
            own[i] += zb_dst[at : at + rows, :].astype(f32)
    xb_src[...] = own[1].astype(bf16)
    second_cross = send(xb_src, xb_dst, device(0, 1))
    far_cross.wait_recv()
    last.extend([along_first(2), along_first(3)])
    second_cross.wait_recv()
    out_ref[:, mid:] = (own[0] + xb_dst[...].astype(f32)).astype(bf16)
    arrive(last)
    total = part[0:rows, :mid]
    for i in range(3):
        total += z_dst[i * rows : (i + 1) * rows, :].astype(f32)
    out_ref[:, :mid] = total.astype(bf16)

    for copy in started:
        copy.wait_send()


def gathered_device(tokens, norm_gain, expert_ids, gate_values, w_gate, w_up, w_down):
    rows, width = tokens.shape
    top = expert_ids.shape[1]
    hidden = w_gate.shape[2]
    every = rows * 16
    bf16, f32 = jnp.bfloat16, jnp.float32
    vmem, hbm = pl.BlockSpec(memory_space=pltpu.VMEM), pl.BlockSpec(memory_space=pl.ANY)
    copies, mid = 29, width * FIRST // 8
    tail = width - mid
    return pl.pallas_call(
        gathered_kernel,
        out_shape=jax.ShapeDtypeStruct((rows, width), bf16),
        in_specs=[hbm] * 7,
        out_specs=vmem,
        scratch_shapes=[
            pltpu.VMEM((rows, width), bf16),
            pltpu.VMEM((1, width), f32),
            pltpu.VMEM((top, rows), jnp.int32),
            pltpu.VMEM((top, rows), f32),
            pltpu.VMEM((every, GATE + width), bf16),
            pltpu.VMEM((width, hidden), bf16),
            pltpu.VMEM((width, hidden), bf16),
            pltpu.VMEM((width, hidden), bf16),
            pltpu.VMEM((every, hidden), bf16),
            pltpu.VMEM((every // 2, width), f32),
            pltpu.VMEM((every // 2, width), bf16),
            pltpu.VMEM((every // 2, width), bf16),
            pltpu.VMEM((every // 4, mid), bf16),
            pltpu.VMEM((every // 4, mid), bf16),
            pltpu.VMEM((3 * rows, mid), bf16),
            pltpu.VMEM((3 * rows, mid), bf16),
            pltpu.VMEM((6 * rows, tail), bf16),
            pltpu.VMEM((6 * rows, tail), bf16),
            pltpu.VMEM((rows, tail), bf16),
            pltpu.VMEM((rows, tail), bf16),
            pltpu.SemaphoreType.DMA((4,)),
            pltpu.SemaphoreType.DMA((3, 4)),
            pltpu.SemaphoreType.DMA((copies,)),
            pltpu.SemaphoreType.DMA((copies,)),
        ],
        compiler_params=pltpu.CompilerParams(
            collective_id=0, has_side_effects=True, vmem_limit_bytes=61 * 1024 * 1024
        ),
    )(tokens, norm_gain.reshape(1, width), expert_ids.T, gate_values.T, w_gate, w_up, w_down)


def solution(mesh):
    in_specs = (
        P(("groups", "expert", "head"), None),
        P(),
        P(("groups", "expert", "head"), None),
        P(("groups", "expert", "head"), None),
        P("expert", None, "head"),
        P("expert", None, "head"),
        P("expert", None, "head"),
    )
    out_specs = P(("groups", "expert", "head"), None)
    experts = mesh.shape["expert"]
    dense = mesh.shape["head"] == 1 and experts == 16
    per_device = gathered_device if dense else routed_device
    return jax.shard_map(
        per_device, mesh=mesh, in_specs=in_specs, out_specs=out_specs, check_vma=False
    )
```
